512 devices in a mesh: island: 32 (over z_hi, y, core), tensor: 16 (over z_lo, x).
Axes of the slice: x: 4, y: 4, z: 16 (z_hi: 4, z_lo: 4; z = z_hi * 4 + z_lo), core: 2. Of those that a mesh axis runs over, the one named last changes fastest.
Arguments:
- grad_slab: bfloat16 [32, 28672, 384], P('island', 'tensor'), may hold values from -3 to 3
- projector: bfloat16 [28672, 512], P('tensor'), may hold values from -0.25 to 0.25
- first_moment: float32 [32, 512, 384], P('island', 'tensor'), may hold values from -3 to 3
- second_moment: float32 [32, 512, 384], P('island', 'tensor'), may hold values from 0.1 to 1
- momentum: float32 [512, 384], P('tensor'), may hold values from -0.9 to 0.9
Outputs:
- update: bfloat16 [28672, 384], P('tensor')
- velocity: float32 [512, 384], P('tensor')
The draws below stay inside these ranges and needn't reach their ends.
All inputs are finite; a program needn't handle non-finite values.
Results may differ from the reference program's by a relative error of at most 0.0049.
Values may be sent and summed in bfloat16 or wider, within the bound.
A program may use at most 64 MiB of HBM per device.

```python
import math
import jax
import jax.numpy as jnp
from jax import lax

FF = 28672
R = 512
COLS = 384
ISL = 32


def shard_levels(key, shape, split, smallest, largest):
    factor_of = 1.0
    for axis_at, blocks in split:
        heights = jax.random.uniform(jax.random.fold_in(jax.random.fold_in(key, 6), axis_at), (blocks,), jnp.float32, smallest / len(split), largest / len(split))
        factor_of = factor_of * jnp.repeat(jnp.exp(heights), shape[axis_at] // blocks).reshape((-1,) + (1,) * (len(shape) - 1 - axis_at))
    return factor_of


def centred(key, shape, scale, most, cuts=(), held_as=jnp.bfloat16):
    entries = jax.random.normal(key, shape, jnp.float32) * scale
    if len(cuts) > 0:
        entries = shard_levels(key, shape, cuts, -0.22, 0.18) * entries
    return jnp.clip(entries, min=-most, max=most).astype(held_as)


def setup_inputs(seed: int = 0) -> dict:
    streams_of = jax.random.split(jax.random.key(seed), 6)
    return {
        "grad_slab": centred(streams_of[0], (ISL, FF, COLS), 0.5, 3.0, ((0, 32), (1, 16))),
        "projector": centred(streams_of[1], (FF, R), R ** -0.5, 0.25, ((0, 16),)),
        "first_moment": centred(streams_of[2], (ISL, R, COLS), 0.5, 3.0, ((0, 32), (1, 16)), jnp.float32),
        "second_moment": jnp.clip(jnp.exp(math.log(1.0) - 2.3025851 * jax.random.uniform(streams_of[3], (ISL, R, COLS), jnp.float32) ** shard_levels(streams_of[3], (ISL, R, COLS), ((0, 32), (1, 16)), -0.2, 0.2)), 0.1, 1.0),
        "momentum": centred(streams_of[4], (R, COLS), 0.15, 0.9, ((0, 16),), jnp.float32),
    }


BETA_ONE = 0.9
BETA_TWO = 0.95
EPSILON = 1e-08
NESTEROV = 0.9
OUTER_RATE = 0.7

def reference(grad_slab, projector, first_moment, second_moment, momentum):

    def replica_step(items):
        gradient, first_old, second_old = items
        projected = lax.dot_general(projector, gradient, (((0,), (0,)), ((), ())), preferred_element_type=jnp.float32)
        first = BETA_ONE * first_old + (1.0 - BETA_ONE) * projected
        second = BETA_TWO * second_old + (1.0 - BETA_TWO) * projected * projected
        return first / (jnp.sqrt(second) + EPSILON)
    pseudo = lax.map(replica_step, (grad_slab, first_moment, second_moment))
    averaged = lax.optimization_barrier(jnp.sum(pseudo, axis=0)) / ISL
    velocity = NESTEROV * momentum + averaged
    outer_step = (averaged + NESTEROV * velocity).astype(jnp.bfloat16)
    update = (OUTER_RATE * jnp.dot(projector, outer_step, preferred_element_type=jnp.float32)).astype(jnp.bfloat16)
    return (update, velocity)
```

```python
import functools

import jax
import jax.numpy as jnp
from jax import lax
from jax.experimental import pallas as pl
from jax.experimental.pallas import tpu as pltpu
from jax.sharding import PartitionSpec as P

BETA_ONE = 0.9
BETA_TWO = 0.95
EPSILON = 1e-08
NESTEROV = 0.9
OUTER_RATE = 0.7
MESH = pl.DeviceIdType.MESH
BF16 = jnp.bfloat16
F32 = jnp.float32

NX, NL, NY, NH, NC = 4, 4, 4, 4, 2
ORDER = (2, 1, 3, 0)


def exchange_kernel(
    grad, proj, first_in, second_in, momentum_in, out, avg_out,
    gv, pv, fm, sm, mom, part, rsbuf, half, corebuf, ybuf, hbuf, og, av,
    load_sem, rs_send, rs_recv, core_sem, y_send, y_recv, h_send, h_recv, ag_send, ag_recv, fw_send, fw_recv, av_sem, out_sem,
):
    rows = fm.shape[1]
    hrows = rows // 2
    tensor = lax.axis_index("tensor")
    island = lax.axis_index("island")
    mx, ml = lax.rem(tensor, NX), lax.div(tensor, NX)
    mc = lax.rem(island, NC)
    my = lax.rem(lax.div(island, NC), NY)
    mh = lax.div(island, NC * NY)
    other = 1 - mc

    def tensor_at(dl, dx):
        return lax.rem(ml + dl, NL) * NX + lax.rem(mx + dx, NX)

    def island_at(dh, dy):
        return (lax.rem(mh + dh, NH) * NY + lax.rem(my + dy, NY)) * NC + mc

    sibling = (island - mc + other, tensor)
    tensor_offsets = [(dl, dx) for dl in ORDER for dx in range(NX) if (dl, dx) != (0, 0)]

    loads = [pltpu.make_async_copy(grad.at[0], gv, load_sem.at[0])]
    for j, dl in enumerate(ORDER):
        block = lax.rem(ml + dl, NL)
        width = NX * rows
        loads.append(pltpu.make_async_copy(proj.at[:, pl.ds(pl.multiple_of(block * width, width), width)], pv.at[j], load_sem.at[1 + j]))
    loads.append(pltpu.make_async_copy(first_in, fm, load_sem.at[5]))
    loads.append(pltpu.make_async_copy(second_in, sm, load_sem.at[6]))
    loads.append(pltpu.make_async_copy(momentum_in.at[pl.ds(pl.multiple_of(mc * hrows, hrows), hrows)], mom, load_sem.at[7]))
    for copy in loads:
        copy.start()

    barrier = pltpu.get_barrier_semaphore()
    partners = [(island, tensor_at(dl, dx)) for dl, dx in tensor_offsets]
    partners.append(sibling)
    partners += [(island_at(0, d), tensor) for d in range(1, NY)]
    partners += [(island_at(d, 0), tensor) for d in range(1, NH)]
    for partner in partners:
        pl.semaphore_signal(barrier, inc=1, device_id=partner, device_id_type=MESH)

    sends = []
    loads[0].wait()
    for j, dl in enumerate(ORDER):
        loads[1 + j].wait()
        block = lax.dot_general(pv[j], gv[...], (((0,), (0,)), ((), ())), preferred_element_type=F32)
        part[j] = block.astype(BF16).reshape(NX, rows, block.shape[1])
        if j == 0:
            pl.semaphore_wait(barrier, len(partners))
        for dx in range(NX):
            if (dl, dx) == (0, 0):
                continue
            k = dl * NX + dx
            copy = pltpu.make_async_remote_copy(
                src_ref=part.at[j, lax.rem(mx + dx, NX)], dst_ref=rsbuf.at[k],
                send_sem=rs_send.at[k], recv_sem=rs_recv.at[k],
                device_id=(island, tensor_at(dl, dx)), device_id_type=MESH)
            copy.start()
            sends.append(copy)
    total = part[len(ORDER) - 1, mx].astype(F32)
    for k, copy in enumerate(sends):
        dl, dx = tensor_offsets[k]
        copy.wait_recv()
        total = total + rsbuf[dl * NX + dx].astype(F32)

    loads[5].wait()
    loads[6].wait()
    first = BETA_ONE * fm[0] + (1.0 - BETA_ONE) * total
    second = BETA_TWO * sm[0] + (1.0 - BETA_TWO) * total * total
    pseudo = first / (jnp.sqrt(second) + EPSILON)
    half[0] = pseudo[:hrows]
    half[1] = pseudo[hrows:]

    copy = pltpu.make_async_remote_copy(
        src_ref=half.at[other], dst_ref=corebuf, send_sem=core_sem.at[0], recv_sem=core_sem.at[1],
        device_id=sibling, device_id_type=MESH)
    copy.start()
    sends.append(copy)
    copy.wait_recv()
    summed = half[mc] + corebuf[...]

    for buf, send, recv, n, me, at in (
        (ybuf, y_send, y_recv, NY, my, lambda d: island_at(0, d)),
        (hbuf, h_send, h_recv, NH, mh, lambda d: island_at(d, 0)),
    ):
        buf[me] = summed.astype(BF16)
        copies = []
        for d in (2, 1, 3):
            copy = pltpu.make_async_remote_copy(
                src_ref=buf.at[me], dst_ref=buf.at[me], send_sem=send.at[d], recv_sem=recv.at[d],
                device_id=(at(d), tensor), device_id_type=MESH)
            copy.start()
            copies.append(copy)
        for copy in copies:
            copy.wait_recv()
        sends += copies
        summed = buf[0].astype(F32)
        for d in range(1, n):
            summed = summed + buf[d].astype(F32)

    averaged = summed / (NH * NY * NC)
    loads[7].wait()
    velocity = NESTEROV * mom[...] + averaged
    og[tensor, mc] = (averaged + NESTEROV * velocity).astype(BF16)
    av[mc] = velocity

    gathers = []
    for dl, dx in tensor_offsets:
        k = dl * NX + dx
        copy = pltpu.make_async_remote_copy(
            src_ref=og.at[tensor, mc], dst_ref=og.at[tensor, mc], send_sem=ag_send.at[k], recv_sem=ag_recv.at[k],
            device_id=(island, tensor_at(dl, dx)), device_id_type=MESH)
        copy.start()
        gathers.append(copy)
    forwards = [
        pltpu.make_async_remote_copy(
            src_ref=av.at[mc], dst_ref=av.at[mc], send_sem=av_sem.at[0], recv_sem=av_sem.at[1],
            device_id=sibling, device_id_type=MESH),
        pltpu.make_async_remote_copy(
            src_ref=og.at[tensor, mc], dst_ref=og.at[tensor, mc], send_sem=fw_send.at[0], recv_sem=fw_recv.at[0],
            device_id=sibling, device_id_type=MESH),
    ]
    for copy in forwards:
        copy.start()
    for copy, (dl, dx) in zip(gathers, tensor_offsets):
        copy.wait_recv()
        source = tensor_at(NL - dl, NX - dx)
        k = dl * NX + dx
        forward = pltpu.make_async_remote_copy(
            src_ref=og.at[source, mc], dst_ref=og.at[source, mc], send_sem=fw_send.at[k], recv_sem=fw_recv.at[k],
            device_id=sibling, device_id_type=MESH)
        forward.start()
        forwards.append(forward)
    for copy in forwards:
        copy.wait_recv()
    stores = [pltpu.make_async_copy(og, out, out_sem.at[0]), pltpu.make_async_copy(av, avg_out, out_sem.at[1])]
    for copy in stores:
        copy.start()
    for copy in sends + gathers + forwards:
        copy.wait_send()
    for copy in stores:
        copy.wait()


def update_kernel(proj, step, update):
    update[...] = (OUTER_RATE * jnp.dot(proj[...], step[...], preferred_element_type=F32)).astype(BF16)


def local(grad_slab, projector, first_moment, second_moment, momentum):
    ff, ranks = projector.shape
    cols = grad_slab.shape[2]
    rows = first_moment.shape[1]
    hrows = rows // 2
    n = NX * NL
    any_spec = pl.BlockSpec(memory_space=pl.ANY)
    dma = pltpu.SemaphoreType.DMA
    step, velocity = pl.pallas_call(
        exchange_kernel,
        name="exchange",
        out_shape=(jax.ShapeDtypeStruct((n, NC, hrows, cols), BF16), jax.ShapeDtypeStruct((NC, hrows, cols), F32)),
        in_specs=[any_spec] * 5,
        out_specs=(any_spec, any_spec),
        scratch_shapes=[
            pltpu.VMEM((ff, cols), BF16),
            pltpu.VMEM((NL, ff, NX * rows), BF16),
            pltpu.VMEM((1, rows, cols), F32),
            pltpu.VMEM((1, rows, cols), F32),
            pltpu.VMEM((hrows, cols), F32),
            pltpu.VMEM((NL, NX, rows, cols), BF16),
            pltpu.VMEM((n, rows, cols), BF16),
            pltpu.VMEM((NC, hrows, cols), F32),
            pltpu.VMEM((hrows, cols), F32),
            pltpu.VMEM((NY, hrows, cols), BF16),
            pltpu.VMEM((NH, hrows, cols), BF16),
            pltpu.VMEM((n, NC, hrows, cols), BF16),
            pltpu.VMEM((NC, hrows, cols), F32),
            dma((8,)), dma((n,)), dma((n,)), dma((2,)), dma((NY,)), dma((NY,)), dma((NH,)), dma((NH,)),
            dma((n,)), dma((n,)), dma((n,)), dma((n,)), dma((2,)), dma((2,)),
        ],
        compiler_params=pltpu.CompilerParams(collective_id=1, has_side_effects=True, vmem_limit_bytes=24 << 20),
    )(grad_slab, projector, first_moment, second_moment, momentum)
    block = 448
    update = pl.pallas_call(
        update_kernel,
        name="update",
        grid=(ff // block,),
        out_shape=jax.ShapeDtypeStruct((ff, cols), BF16),
        in_specs=[pl.BlockSpec((block, ranks), lambda i: (i, 0)), pl.BlockSpec((ranks, cols), lambda i: (0, 0))],
        out_specs=pl.BlockSpec((block, cols), lambda i: (i, 0)),
        compiler_params=pltpu.CompilerParams(vmem_limit_bytes=16 << 20),
    )(projector, step.reshape(ranks, cols))
    return (update, velocity.reshape(rows, cols))


def solution(mesh):
    in_specs = (
        P("island", "tensor", None),
        P("tensor", None),
        P("island", "tensor", None),
        P("island", "tensor", None),
        P("tensor", None),
    )
    out_specs = (P("tensor", None), P("tensor", None))
    return jax.shard_map(local, mesh=mesh, in_specs=in_specs, out_specs=out_specs, check_vma=False)
```

```python
import jax
import jax.numpy as jnp
from jax import lax
from jax.experimental import pallas as pl
from jax.experimental.pallas import tpu as pltpu
from jax.sharding import PartitionSpec as P

BETA_ONE = 0.9
BETA_TWO = 0.95
EPSILON = 1e-08
NESTEROV = 0.9
OUTER_RATE = 0.7
MESH = pl.DeviceIdType.MESH
BF16 = jnp.bfloat16
F32 = jnp.float32

NX, NL, NY, NH, NC = 4, 4, 4, 4, 2
NZ = NH * NL
LPC = NL // NC
ORDER = (2, 1, 3, 0)


def exchange_kernel(
    grad, proj, first_in, second_in, momentum_in, step_out, velocity_out,
    gv, pv, fm, sm, part, xbuf, lsend, lbuf, pse, ybuf, chunk, zbuf, mombuf, vel, vout, og,
    load_sem, x_send, x_recv, l_send, l_recv, y_send, y_recv, m_send, m_recv, z_send, z_recv,
    v_send, v_recv, g_send, g_recv, f_send, f_recv, out_sem,
):
    rows = fm.shape[1]
    group = rows // NY
    width = NX * rows
    tensor = lax.axis_index("tensor")
    island = lax.axis_index("island")
    mx, ml = lax.rem(tensor, NX), lax.div(tensor, NX)
    mc = lax.rem(island, NC)
    my = lax.rem(lax.div(island, NC), NY)
    mh = lax.div(island, NC * NY)
    mz = mh * NL + ml
    sigma = lax.div(ml, LPC)
    active = mc == sigma
    li = lax.rem(ml, LPC)

    def device(x=mx, y=my, z=mz, c=mc):
        return ((lax.div(z, NL) * NY + y) * NC + c, lax.rem(z, NL) * NX + x)

    def at_x(d):
        return lax.rem(mx + d, NX)

    def at_y(d):
        return lax.rem(my + d, NY)

    def at_l(d):
        return lax.rem(ml + d, NL)

    def at_z(d):
        return lax.rem(mz + d, NZ)

    sibling = device(c=1 - mc)
    xy_offsets = [(dx, dy) for dx in (2, 1, 3, 0) for dy in (2, 1, 3, 0) if (dx, dy) != (0, 0)]
    z_offsets = (8, 7, 9, 6, 10, 5, 11, 4, 12, 3, 13, 2, 14, 1, 15)

    def remote(src, dst, send, recv, to):
        return pltpu.make_async_remote_copy(
            src_ref=src, dst_ref=dst, send_sem=send, recv_sem=recv, device_id=to, device_id_type=MESH)

    loads = [pltpu.make_async_copy(grad.at[0], gv, load_sem.at[0])]
    for j, d in enumerate(ORDER):
        ranks = pl.ds(pl.multiple_of(at_l(d) * width, width), width)
        loads.append(pltpu.make_async_copy(proj.at[:, ranks], pv.at[j], load_sem.at[1 + j]))
    loads.append(pltpu.make_async_copy(first_in, fm, load_sem.at[5]))
    loads.append(pltpu.make_async_copy(second_in, sm, load_sem.at[6]))
    own_rows = pl.ds(pl.multiple_of(my * group, group), group)
    loads.append(pltpu.make_async_copy(momentum_in.at[own_rows], vel.at[0], load_sem.at[7]))
    for copy in loads:
        copy.start()

    barrier = pltpu.get_barrier_semaphore()
    partners = [device(z=at_z(d)) for d in z_offsets]
    partners += [device(x=at_x(dx), y=at_y(dy)) for dx, dy in xy_offsets]
    partners += [device(y=at_y(d), c=1 - mc) for d in range(NY)]
    for partner in partners:
        pl.semaphore_signal(barrier, inc=1, device_id=partner, device_id_type=MESH)

    x_copies = []
    loads[0].wait()
    for j, d in enumerate(ORDER):
        loads[1 + j].wait()
        block = lax.dot_general(pv[j], gv[...], (((0,), (0,)), ((), ())), preferred_element_type=F32)
        part[j] = block.astype(BF16).reshape(NX, rows, block.shape[1])
        if j == 0:
            pl.semaphore_wait(barrier, len(partners))
        for dx in (2, 1, 3):
            copy = remote(part.at[j, at_x(dx)], xbuf.at[j, dx - 1], x_send.at[j, dx - 1], x_recv.at[j, dx - 1], device(x=at_x(dx)))
            copy.start()
            x_copies.append(copy)

    loads[7].wait()
    vel[1] = vel[0]

    @pl.when(active)
    def _():
        pltpu.make_async_copy(vel.at[1], mombuf.at[li], m_recv.at[li]).start()
        for d in range(1, NL):
            remote(vel.at[1], mombuf.at[li], m_send.at[d], m_recv.at[li], device(z=mz - ml + at_l(d))).start()

    l_copies = []
    total = None
    for j, d in enumerate(ORDER):
        for k in range(3):
            x_copies[3 * j + k].wait_recv()
        total = part[j, mx].astype(F32)
        for k in range(3):
            total = total + xbuf[j, k].astype(F32)
        if d:
            lsend[j] = total.astype(BF16)
            copy = remote(lsend.at[j], lbuf.at[j], l_send.at[j], l_recv.at[j], device(z=mz - ml + at_l(d)))
            copy.start()
            l_copies.append(copy)
    loads[5].wait()
    loads[6].wait()
    for j in range(NL - 1):
        l_copies[j].wait_recv()
        total = total + lbuf[j].astype(F32)

    first = BETA_ONE * fm[0] + (1.0 - BETA_ONE) * total
    second = BETA_TWO * sm[0] + (1.0 - BETA_TWO) * total * total
    pseudo = first / (jnp.sqrt(second) + EPSILON)
    pse[...] = pseudo.reshape(pse.shape)

    slot = mc * NY + my
    y_copies = []
    for d in (2, 1, 3):
        copy = remote(pse.at[at_y(d)], ybuf.at[slot], y_send.at[d], y_recv.at[slot], device(y=at_y(d), c=sigma))
        copy.start()
        y_copies.append(copy)
    to_sibling = remote(pse.at[my], ybuf.at[slot], y_send.at[0], y_recv.at[slot], sibling)

    @pl.when(jnp.logical_not(active))
    def _():
        to_sibling.start()

    @pl.when(active)
    def _():
        pltpu.make_async_copy(pse.at[my], ybuf.at[slot], y_recv.at[slot]).start()
        for s in range(NC * NY):
            pltpu.make_async_copy(pse.at[0], ybuf.at[s], y_recv.at[s]).wait()
        summed = ybuf[0]
        for s in range(1, NC * NY):
            summed = summed + ybuf[s]
        chunk[...] = summed.astype(BF16)
        for k, d in enumerate(z_offsets):
            remote(chunk, zbuf.at[mh, li], z_send.at[k], z_recv.at[mh, li], device(z=at_z(d))).start()
        pltpu.make_async_copy(chunk, zbuf.at[mh, li], z_recv.at[mh, li]).start()

    for i in range(LPC):
        pltpu.make_async_copy(vel.at[1], mombuf.at[i], m_recv.at[i]).wait()
    for h in range(NH):
        for i in range(LPC):
            pltpu.make_async_copy(chunk, zbuf.at[h, i], z_recv.at[h, i]).wait()
    summed = zbuf[0].astype(F32)
    for h in range(1, NH):
        summed = summed + zbuf[h].astype(F32)
    averaged = summed / (NH * NY * NC)
    velocity = NESTEROV * mombuf[...] + averaged
    outer_step = (averaged + NESTEROV * velocity).astype(BF16)
    half = pl.ds(mc * LPC, LPC)
    og[half, mx, my] = outer_step
    vel[2:] = velocity

    g_copies = []
    for k, (dx, dy) in enumerate(xy_offsets):
        copy = remote(og.at[half, mx, my], og.at[half, mx, my], g_send.at[k], g_recv.at[k], device(x=at_x(dx), y=at_y(dy)))
        copy.start()
        g_copies.append(copy)
    f_copies = [remote(og.at[half, mx, my], og.at[half, mx, my], f_send.at[NX * NY - 1], f_recv.at[NX * NY - 1], sibling)]
    f_copies[0].start()

    @pl.when(active)
    def _():
        pltpu.make_async_copy(vel.at[2 + li], vout.at[my], v_recv.at[my]).start()
        for d in range(1, NY):
            for c in range(NC):
                remote(vel.at[2 + li], vout.at[my], v_send.at[d, c], v_recv.at[my], device(y=at_y(d), c=c)).start()
        remote(vel.at[2 + li], vout.at[my], v_send.at[0, 0], v_recv.at[my], sibling).start()

    for k, (dx, dy) in enumerate(xy_offsets):
        g_copies[k].wait_recv()
        src = og.at[half, at_x(NX - dx), at_y(NY - dy)]
        copy = remote(src, src, f_send.at[k], f_recv.at[k], sibling)
        copy.start()
        f_copies.append(copy)
    for copy in f_copies:
        copy.wait_recv()
    for y in range(NY):
        pltpu.make_async_copy(vel.at[2], vout.at[y], v_recv.at[y]).wait()
    stores = [pltpu.make_async_copy(og, step_out, out_sem.at[0]), pltpu.make_async_copy(vout, velocity_out, out_sem.at[1])]
    for copy in stores:
        copy.start()
    for copy in x_copies + l_copies + y_copies + g_copies + f_copies:
        copy.wait_send()

    @pl.when(jnp.logical_not(active))
    def _():
        to_sibling.wait_send()

    @pl.when(active)
    def _():
        for d in range(1, NL):
            remote(vel.at[1], mombuf.at[li], m_send.at[d], m_recv.at[li], sibling).wait_send()
        for k in range(NZ - 1):
            remote(chunk, zbuf.at[mh, li], z_send.at[k], z_recv.at[mh, li], sibling).wait_send()
        for d in range(1, NY):
            for c in range(NC):
                remote(vel.at[2], vout.at[my], v_send.at[d, c], v_recv.at[my], sibling).wait_send()
        remote(vel.at[2], vout.at[my], v_send.at[0, 0], v_recv.at[my], sibling).wait_send()

    for copy in stores:
        copy.wait()


def update_kernel(proj, step, update):
    update[...] = (OUTER_RATE * jnp.dot(proj[...], step[...], preferred_element_type=F32)).astype(BF16)


def exchange(grad_slab, projector, first_moment, second_moment, momentum):
    ff = projector.shape[0]
    cols = grad_slab.shape[2]
    rows = first_moment.shape[1]
    group = rows // NY
    any_spec = pl.BlockSpec(memory_space=pl.ANY)
    hbm_spec = pl.BlockSpec(memory_space=pltpu.HBM)
    dma = pltpu.SemaphoreType.DMA
    return pl.pallas_call(
        exchange_kernel,
        name="exchange",
        out_shape=(
            jax.ShapeDtypeStruct((NL, NX, NY, group, cols), BF16),
            jax.ShapeDtypeStruct((NY, group, cols), F32),
        ),
        in_specs=[hbm_spec] * 5,
        out_specs=(any_spec, any_spec),
        scratch_shapes=[
            pltpu.VMEM((ff, cols), BF16),
            pltpu.VMEM((NL, ff, NX * rows), BF16),
            pltpu.VMEM((1, rows, cols), F32),
            pltpu.VMEM((1, rows, cols), F32),
            pltpu.VMEM((NL, NX, rows, cols), BF16),
            pltpu.VMEM((NL, NX - 1, rows, cols), BF16),
            pltpu.VMEM((NL - 1, rows, cols), BF16),
            pltpu.VMEM((NL - 1, rows, cols), BF16),
            pltpu.VMEM((NY, group, cols), F32),
            pltpu.VMEM((NC * NY, group, cols), F32),
            pltpu.VMEM((group, cols), BF16),
            pltpu.VMEM((NH, LPC, group, cols), BF16),
            pltpu.VMEM((LPC, group, cols), F32),
            pltpu.VMEM((2 + LPC, group, cols), F32),
            pltpu.VMEM((NY, group, cols), F32),
            pltpu.VMEM((NL, NX, NY, group, cols), BF16),
            dma((8,)),
            dma((NL, NX - 1)), dma((NL, NX - 1)),
            dma((NL - 1,)), dma((NL - 1,)),
            dma((NY,)), dma((NC * NY,)),
            dma((NL,)), dma((LPC,)),
            dma((NZ - 1,)), dma((NH, LPC)),
            dma((NY, NC)), dma((NY,)),
            dma((NX * NY - 1,)), dma((NX * NY - 1,)),
            dma((NX * NY,)), dma((NX * NY,)),
            dma((2,)),
        ],
        compiler_params=pltpu.CompilerParams(collective_id=1, has_side_effects=True, vmem_limit_bytes=24 << 20),
    )(*[pltpu.with_memory_space_constraint(a, pltpu.HBM) for a in (grad_slab, projector, first_moment, second_moment, momentum)])


def local(grad_slab, projector, first_moment, second_moment, momentum):
    ff, ranks = projector.shape
    cols = grad_slab.shape[2]
    rows = first_moment.shape[1]
    step, velocity = exchange(grad_slab, projector, first_moment, second_moment, momentum)
    block = 448
    update = pl.pallas_call(
        update_kernel,
        name="update",
        grid=(ff // block,),
        out_shape=jax.ShapeDtypeStruct((ff, cols), BF16),
        in_specs=[pl.BlockSpec((block, ranks), lambda i: (i, 0)), pl.BlockSpec((ranks, cols), lambda i: (0, 0))],
        out_specs=pl.BlockSpec((block, cols), lambda i: (i, 0)),
        compiler_params=pltpu.CompilerParams(vmem_limit_bytes=16 << 20),
    )(projector, step.reshape(ranks, cols))
    return (update, velocity.reshape(rows, cols))


def solution(mesh):
    in_specs = (
        P("island", "tensor", None),
        P("tensor", None),
        P("island", "tensor", None),
        P("island", "tensor", None),
        P("tensor", None),
    )
    out_specs = (P("tensor", None), P("tensor", None))
    return jax.shard_map(local, mesh=mesh, in_specs=in_specs, out_specs=out_specs, check_vma=False)
```

```python
import jax
import jax.numpy as jnp
from jax import lax
from jax.experimental import pallas as pl
from jax.experimental.pallas import tpu as pltpu
from jax.sharding import PartitionSpec as P

BETA_ONE = 0.9
BETA_TWO = 0.95
EPSILON = 1e-08
NESTEROV = 0.9
OUTER_RATE = 0.7
MESH = pl.DeviceIdType.MESH
BF16 = jnp.bfloat16
F32 = jnp.float32

NX, NL, NY, NH, NC = 4, 4, 4, 4, 2
NZ = NH * NL
LPC = NL // NC
REACH = 4
UPDATE_ROWS = 256


def exchange_kernel(
    grad, proj, first_in, second_in, momentum_in, pv, og, vout,
    gv, fm, sm, part, xbuf, lsend, lbuf, pse, ybuf, chunk, zbuf, mombuf, vel,
    load_sem, x_send, x_recv, l_send, l_recv, y_send, y_recv, m_send, m_recv, z_send, z_recv,
    v_send, v_recv, g_send, g_recv, f_send, f_recv, ring_sem,
):
    rows = fm.shape[1]
    group = rows // NY
    width = NX * rows
    tensor = lax.axis_index("tensor")
    island = lax.axis_index("island")
    mx, ml = lax.rem(tensor, NX), lax.div(tensor, NX)
    mc = lax.rem(island, NC)
    my = lax.rem(lax.div(island, NC), NY)
    mh = lax.div(island, NC * NY)
    mz = mh * NL + ml
    sigma = lax.div(ml, LPC)
    active = mc == sigma
    li = lax.rem(ml, LPC)

    def device(x=mx, y=my, z=mz, c=mc):
        return ((lax.div(z, NL) * NY + y) * NC + c, lax.rem(z, NL) * NX + x)

    def at_x(d):
        return lax.rem(mx + d, NX)

    def at_y(d):
        return lax.rem(my + d, NY)

    def at_l(d):
        return lax.rem(ml + d, NL)

    def at_z(d):
        return lax.rem(mz + d, NZ)

    farthest = jnp.where(ml < 2, 3, 0)
    nearer = 1 + lax.rem(ml, 2)
    order = (farthest, 6 - ml - farthest - nearer, nearer, ml)
    sibling = device(c=1 - mc)
    xy_offsets = [(dx, dy) for dx in (2, 1, 3, 0) for dy in (2, 1, 3, 0) if (dx, dy) != (0, 0)]
    z_offsets = (8, 7, 9, 6, 10, 5, 11, 4, 12, 3, 13, 2, 14, 1, 15)

    def remote(src, dst, send, recv, to):
        return pltpu.make_async_remote_copy(
            src_ref=src, dst_ref=dst, send_sem=send, recv_sem=recv, device_id=to, device_id_type=MESH)

    loads = [pltpu.make_async_copy(grad.at[0], gv, load_sem.at[0])]
    ranks = [pl.ds(pl.multiple_of(block * width, width), width) for block in order]
    for j in range(NL):
        loads.append(pltpu.make_async_copy(proj.at[:, ranks[j]], pv.at[:, ranks[j]], load_sem.at[1 + j]))
    loads.append(pltpu.make_async_copy(first_in, fm, load_sem.at[5]))
    loads.append(pltpu.make_async_copy(second_in, sm, load_sem.at[6]))
    own_rows = pl.ds(pl.multiple_of(my * group, group), group)
    loads.append(pltpu.make_async_copy(momentum_in.at[own_rows], vel.at[0], load_sem.at[7]))
    for copy in loads:
        copy.start()

    barrier = pltpu.get_barrier_semaphore()
    partners = [device(z=at_z(d)) for d in z_offsets if min(d, NZ - d) <= REACH]
    partners += [device(x=at_x(dx), y=at_y(dy)) for dx, dy in xy_offsets]
    partners += [device(y=at_y(d), c=1 - mc) for d in range(NY)]
    for partner in partners:
        pl.semaphore_signal(barrier, inc=1, device_id=partner, device_id_type=MESH)

    x_copies = []
    loads[0].wait()
    for j in range(NL):
        loads[1 + j].wait()
        block = lax.dot_general(pv[:, ranks[j]], gv[...], (((0,), (0,)), ((), ())), preferred_element_type=F32)
        part[j] = block.astype(BF16).reshape(NX, rows, block.shape[1])
        if j == 0:
            pl.semaphore_wait(barrier, len(partners))
            for d in (REACH, NZ - REACH):
                pl.semaphore_signal(ring_sem, inc=1, device_id=device(z=at_z(d)), device_id_type=MESH)
        for dx in (2, 1, 3):
            copy = remote(part.at[j, at_x(dx)], xbuf.at[j, dx - 1], x_send.at[j, dx - 1], x_recv.at[j, dx - 1], device(x=at_x(dx)))
            copy.start()
            x_copies.append(copy)

    loads[7].wait()
    vel[1] = vel[0]

    @pl.when(active)
    def _():
        pltpu.make_async_copy(vel.at[1], mombuf.at[li], m_recv.at[li]).start()
        for d in range(1, NL):
            remote(vel.at[1], mombuf.at[li], m_send.at[d], m_recv.at[li], device(z=mz - ml + at_l(d))).start()

    l_copies = []
    total = None
    for j in range(NL):
        for k in range(3):
            x_copies[3 * j + k].wait_recv()
        total = part[j, mx].astype(F32)
        for k in range(3):
            total = total + xbuf[j, k].astype(F32)
        if j < NL - 1:
            lsend[j] = total.astype(BF16)
            copy = remote(lsend.at[j], lbuf.at[ml], l_send.at[j], l_recv.at[ml], device(z=mz - ml + order[j]))
            copy.start()
            l_copies.append(copy)
    loads[5].wait()
    loads[6].wait()
    for d in range(1, NL):
        pltpu.make_async_copy(lsend.at[0], lbuf.at[at_l(d)], l_recv.at[at_l(d)]).wait()
        total = total + lbuf[at_l(d)].astype(F32)

    first = BETA_ONE * fm[0] + (1.0 - BETA_ONE) * total
    second = BETA_TWO * sm[0] + (1.0 - BETA_TWO) * total * total
    pseudo = first / (jnp.sqrt(second) + EPSILON)
    pse[...] = pseudo.reshape(pse.shape)

    slot = mc * NY + my
    y_copies = []
    for d in (2, 1, 3):
        copy = remote(pse.at[at_y(d)], ybuf.at[slot], y_send.at[d], y_recv.at[slot], device(y=at_y(d), c=sigma))
        copy.start()
        y_copies.append(copy)
    to_sibling = remote(pse.at[my], ybuf.at[slot], y_send.at[0], y_recv.at[slot], sibling)

    @pl.when(jnp.logical_not(active))
    def _():
        to_sibling.start()

    pl.semaphore_wait(ring_sem, 2)

    @pl.when(active)
    def _():
        pltpu.make_async_copy(pse.at[my], ybuf.at[slot], y_recv.at[slot]).start()
        for s in range(NC * NY):
            pltpu.make_async_copy(pse.at[0], ybuf.at[s], y_recv.at[s]).wait()
        summed = ybuf[0]
        for s in range(1, NC * NY):
            summed = summed + ybuf[s]
        chunk[...] = summed.astype(BF16)
        for k, d in enumerate(z_offsets):
            remote(chunk, zbuf.at[mh, li], z_send.at[k], z_recv.at[mh, li], device(z=at_z(d))).start()
        pltpu.make_async_copy(chunk, zbuf.at[mh, li], z_recv.at[mh, li]).start()

    for i in range(LPC):
        pltpu.make_async_copy(vel.at[1], mombuf.at[i], m_recv.at[i]).wait()
    for h in range(NH):
        for i in range(LPC):
            pltpu.make_async_copy(chunk, zbuf.at[h, i], z_recv.at[h, i]).wait()
    summed = zbuf[0].astype(F32)
    for h in range(1, NH):
        summed = summed + zbuf[h].astype(F32)
    averaged = summed / (NH * NY * NC)
    velocity = NESTEROV * mombuf[...] + averaged
    outer_step = (averaged + NESTEROV * velocity).astype(BF16)
    half = pl.ds(mc * LPC, LPC)
    og[half, mx, my] = outer_step
    vel[2:] = velocity

    g_copies = []
    for k, (dx, dy) in enumerate(xy_offsets):
        copy = remote(og.at[half, mx, my], og.at[half, mx, my], g_send.at[k], g_recv.at[k], device(x=at_x(dx), y=at_y(dy)))
        copy.start()
        g_copies.append(copy)
    f_copies = [remote(og.at[half, mx, my], og.at[half, mx, my], f_send.at[NX * NY - 1], f_recv.at[NX * NY - 1], sibling)]
    f_copies[0].start()

    @pl.when(active)
    def _():
        pltpu.make_async_copy(vel.at[2 + li], vout.at[my], v_recv.at[my]).start()
        for d in range(1, NY):
            for c in range(NC):
                remote(vel.at[2 + li], vout.at[my], v_send.at[d, c], v_recv.at[my], device(y=at_y(d), c=c)).start()
        remote(vel.at[2 + li], vout.at[my], v_send.at[0, 0], v_recv.at[my], sibling).start()

    for k, (dx, dy) in enumerate(xy_offsets):
        g_copies[k].wait_recv()
        src = og.at[half, at_x(NX - dx), at_y(NY - dy)]
        copy = remote(src, src, f_send.at[k], f_recv.at[k], sibling)
        copy.start()
        f_copies.append(copy)
    for copy in f_copies:
        copy.wait_recv()
    for y in range(NY):
        pltpu.make_async_copy(vel.at[2], vout.at[y], v_recv.at[y]).wait()
    for copy in x_copies + l_copies + y_copies + g_copies + f_copies:
        copy.wait_send()

    @pl.when(jnp.logical_not(active))
    def _():
        to_sibling.wait_send()

    @pl.when(active)
    def _():
        for d in range(1, NL):
            remote(vel.at[1], mombuf.at[li], m_send.at[d], m_recv.at[li], sibling).wait_send()
        for k in range(NZ - 1):
            remote(chunk, zbuf.at[mh, li], z_send.at[k], z_recv.at[mh, li], sibling).wait_send()
        for d in range(1, NY):
            for c in range(NC):
                remote(vel.at[2], vout.at[my], v_send.at[d, c], v_recv.at[my], sibling).wait_send()
        remote(vel.at[2], vout.at[my], v_send.at[0, 0], v_recv.at[my], sibling).wait_send()


def update_kernel(proj, step, velocity, update_out, velocity_out, update, sem):
    blocks = proj.shape[0] // UPDATE_ROWS
    stores = [pltpu.make_async_copy(velocity, velocity_out, sem.at[blocks])]
    stores[0].start()
    for i in range(blocks):
        rows = pl.ds(i * UPDATE_ROWS, UPDATE_ROWS)
        update[rows] = (OUTER_RATE * jnp.dot(proj[rows], step[...], preferred_element_type=F32)).astype(BF16)
        copy = pltpu.make_async_copy(update.at[rows], update_out.at[rows], sem.at[i])
        copy.start()
        stores.append(copy)
    for copy in stores:
        copy.wait()


def exchange(grad_slab, projector, first_moment, second_moment, momentum):
    ff = projector.shape[0]
    cols = grad_slab.shape[2]
    rows = first_moment.shape[1]
    group = rows // NY
    vmem_spec = pl.BlockSpec(memory_space=pltpu.VMEM)
    hbm_spec = pl.BlockSpec(memory_space=pltpu.HBM)
    dma = pltpu.SemaphoreType.DMA
    return pl.pallas_call(
        exchange_kernel,
        name="exchange",
        out_shape=(
            pltpu.VMEM(projector.shape, BF16),
            pltpu.VMEM((NL, NX, NY, group, cols), BF16),
            pltpu.VMEM((NY, group, cols), F32),
        ),
        in_specs=[hbm_spec] * 5,
        out_specs=(vmem_spec,) * 3,
        scratch_shapes=[
            pltpu.VMEM((ff, cols), BF16),
            pltpu.VMEM((1, rows, cols), F32),
            pltpu.VMEM((1, rows, cols), F32),
            pltpu.VMEM((NL, NX, rows, cols), BF16),
            pltpu.VMEM((NL, NX - 1, rows, cols), BF16),
            pltpu.VMEM((NL - 1, rows, cols), BF16),
            pltpu.VMEM((NL, rows, cols), BF16),
            pltpu.VMEM((NY, group, cols), F32),
            pltpu.VMEM((NC * NY, group, cols), F32),
            pltpu.VMEM((group, cols), BF16),
            pltpu.VMEM((NH, LPC, group, cols), BF16),
            pltpu.VMEM((LPC, group, cols), F32),
            pltpu.VMEM((2 + LPC, group, cols), F32),
            dma((8,)),
            dma((NL, NX - 1)), dma((NL, NX - 1)),
            dma((NL - 1,)), dma((NL,)),
            dma((NY,)), dma((NC * NY,)),
            dma((NL,)), dma((LPC,)),
            dma((NZ - 1,)), dma((NH, LPC)),
            dma((NY, NC)), dma((NY,)),
            dma((NX * NY - 1,)), dma((NX * NY - 1,)),
            dma((NX * NY,)), dma((NX * NY,)),
            pltpu.SemaphoreType.REGULAR,
        ],
        compiler_params=pltpu.CompilerParams(collective_id=1, has_side_effects=True, vmem_limit_bytes=24 << 20),
    )(*[pltpu.with_memory_space_constraint(a, pltpu.HBM) for a in (grad_slab, projector, first_moment, second_moment, momentum)])


def local(grad_slab, projector, first_moment, second_moment, momentum):
    ff, ranks = projector.shape
    cols = grad_slab.shape[2]
    rows = first_moment.shape[1]
    proj, step, velocity = exchange(grad_slab, projector, first_moment, second_moment, momentum)
    vmem_spec = pl.BlockSpec(memory_space=pltpu.VMEM)
    any_spec = pl.BlockSpec(memory_space=pl.ANY)
    operands = (proj, step.reshape(ranks, cols), velocity.reshape(rows, cols))
    return pl.pallas_call(
        update_kernel,
        name="update",
        out_shape=(jax.ShapeDtypeStruct((ff, cols), BF16), jax.ShapeDtypeStruct((rows, cols), F32)),
        in_specs=[vmem_spec] * 3,
        out_specs=(any_spec, any_spec),
        scratch_shapes=[pltpu.VMEM((ff, cols), BF16), pltpu.SemaphoreType.DMA((ff // UPDATE_ROWS + 1,))],
        compiler_params=pltpu.CompilerParams(vmem_limit_bytes=16 << 20),
    )(*[pltpu.with_memory_space_constraint(a, pltpu.VMEM) for a in operands])


def solution(mesh):
    in_specs = (
        P("island", "tensor", None),
        P("tensor", None),
        P("island", "tensor", None),
        P("island", "tensor", None),
        P("tensor", None),
    )
    out_specs = (P("tensor", None), P("tensor", None))
    return jax.shard_map(local, mesh=mesh, in_specs=in_specs, out_specs=out_specs, check_vma=False)
```

```python
import jax
import jax.numpy as jnp
from jax import lax
from jax.experimental import pallas as pl
from jax.experimental.pallas import tpu as pltpu
from jax.sharding import PartitionSpec as P

BETA_ONE = 0.9
BETA_TWO = 0.95
EPSILON = 1e-08
NESTEROV = 0.9
OUTER_RATE = 0.7
MESH = pl.DeviceIdType.MESH
BF16 = jnp.bfloat16
F32 = jnp.float32

NX, NL, NY, NH, NC = 4, 4, 4, 4, 2
NZ = NH * NL
LPC = NL // NC
REACH = 2
UPDATE_ROWS = 256


def exchange_kernel(
    grad, proj, first_in, second_in, momentum_in, pv, og, vout,
    gv, fm, sm, part, xbuf, lsend, lbuf, pse, ybuf, chunk, zbuf, mombuf, vel,
    load_sem, x_send, x_recv, l_send, l_recv, y_send, y_recv, m_send, m_recv, z_send, z_recv,
    v_send, v_recv, g_send, g_recv, f_send, f_recv, ring_sem, wide_sem,
):
    rows = fm.shape[1]
    group = rows // NY
    width = NX * rows
    tensor = lax.axis_index("tensor")
    island = lax.axis_index("island")
    mx, ml = lax.rem(tensor, NX), lax.div(tensor, NX)
    mc = lax.rem(island, NC)
    my = lax.rem(lax.div(island, NC), NY)
    mh = lax.div(island, NC * NY)
    mz = mh * NL + ml
    sigma = lax.div(ml, LPC)
    active = mc == sigma
    li = lax.rem(ml, LPC)

    def device(x=mx, y=my, z=mz, c=mc):
        return ((lax.div(z, NL) * NY + y) * NC + c, lax.rem(z, NL) * NX + x)

    def at_x(d):
        return lax.rem(mx + d, NX)

    def at_y(d):
        return lax.rem(my + d, NY)

    def at_l(d):
        return lax.rem(ml + d, NL)

    def at_z(d):
        return lax.rem(mz + d, NZ)

    farthest = jnp.where(ml < 2, 3, 0)
    nearer = 1 + lax.rem(ml, 2)
    order = (farthest, 6 - ml - farthest - nearer, nearer, ml)
    sibling = device(c=1 - mc)
    xy_offsets = sorted(
        [(dx, dy) for dx in range(NX) for dy in range(NY) if (dx, dy) != (0, 0)],
        key=lambda d: -(min(d[0], NX - d[0]) + min(d[1], NY - d[1])))
    z_offsets = (8, 7, 9, 6, 10, 5, 11, 4, 12, 3, 13, 2, 14, 1, 15)

    def remote(src, dst, send, recv, to):
        return pltpu.make_async_remote_copy(
            src_ref=src, dst_ref=dst, send_sem=send, recv_sem=recv, device_id=to, device_id_type=MESH)

    loads = [pltpu.make_async_copy(grad.at[0], gv, load_sem.at[0])]
    ranks = [pl.ds(pl.multiple_of(block * width, width), width) for block in order]
    for j in range(NL):
        loads.append(pltpu.make_async_copy(proj.at[:, ranks[j]], pv.at[:, ranks[j]], load_sem.at[1 + j]))
    loads.append(pltpu.make_async_copy(first_in, fm, load_sem.at[5]))
    loads.append(pltpu.make_async_copy(second_in, sm, load_sem.at[6]))
    own_rows = pl.ds(pl.multiple_of(my * group, group), group)
    loads.append(pltpu.make_async_copy(momentum_in.at[own_rows], vel.at[0], load_sem.at[7]))
    for copy in loads:
        copy.start()

    barrier = pltpu.get_barrier_semaphore()
    partners = [device(z=at_z(d)) for d in z_offsets if min(d, NZ - d) <= REACH]
    partners += [device(x=at_x(d)) for d in range(1, NX)]
    partners += [device(y=at_y(d)) for d in range(1, NY)]
    partners += [device(y=at_y(d), c=1 - mc) for d in range(NY)]
    for partner in partners:
        pl.semaphore_signal(barrier, inc=1, device_id=partner, device_id_type=MESH)

    x_copies = []
    loads[0].wait()
    for j in range(NL):
        loads[1 + j].wait()
        block = lax.dot_general(pv[:, ranks[j]], gv[...], (((0,), (0,)), ((), ())), preferred_element_type=F32)
        block = block.astype(BF16)
        part[j] = block.reshape(part.shape[1:])
        if j == 0:
            pl.semaphore_wait(barrier, len(partners))
            for d in (REACH, NZ - REACH):
                pl.semaphore_signal(ring_sem, inc=1, device_id=device(z=at_z(d)), device_id_type=MESH)
        for dx in (2, 1, 3):
            copy = remote(part.at[j, at_x(dx)], xbuf.at[j, dx - 1], x_send.at[j, dx - 1], x_recv.at[j, dx - 1], device(x=at_x(dx)))
            copy.start()
            x_copies.append(copy)

    pl.semaphore_wait(ring_sem, 2)
    for d in (2 * REACH, NZ - 2 * REACH):
        pl.semaphore_signal(wide_sem, inc=1, device_id=device(z=at_z(d)), device_id_type=MESH)

    loads[7].wait()
    vel[1] = vel[0]

    @pl.when(active)
    def _():
        pltpu.make_async_copy(vel.at[1], mombuf.at[li], m_recv.at[li]).start()
        for d in range(1, NL):
            remote(vel.at[1], mombuf.at[li], m_send.at[d], m_recv.at[li], device(z=mz - ml + at_l(d))).start()

    def over_x(j):
        for k in range(3):
            x_copies[3 * j + k].wait_recv()
        total = part[j, mx].astype(F32)
        for k in range(3):
            total = total + xbuf[j, k].astype(F32)
        return total

    l_copies = []
    for j in range(NL - 1):
        lsend[j] = over_x(j).astype(BF16)
        copy = remote(lsend.at[j], lbuf.at[ml], l_send.at[j], l_recv.at[ml], device(z=mz - ml + order[j]))
        copy.start()
        l_copies.append(copy)
    total = over_x(NL - 1)
    loads[5].wait()
    loads[6].wait()
    for d in range(1, NL):
        pltpu.make_async_copy(lsend.at[0], lbuf.at[at_l(d)], l_recv.at[at_l(d)]).wait()
        total = total + lbuf[at_l(d)].astype(F32)

    first = BETA_ONE * fm[0] + (1.0 - BETA_ONE) * total
    second = BETA_TWO * sm[0] + (1.0 - BETA_TWO) * total * total
    pseudo = first / (jnp.sqrt(second) + EPSILON)
    pse[...] = pseudo.reshape(pse.shape)

    slot = mc * NY + my
    y_copies = []
    for d in (2, 1, 3):
        copy = remote(pse.at[at_y(d)], ybuf.at[slot], y_send.at[d], y_recv.at[slot], device(y=at_y(d), c=sigma))
        copy.start()
        y_copies.append(copy)
    to_sibling = remote(pse.at[my], ybuf.at[slot], y_send.at[0], y_recv.at[slot], sibling)

    @pl.when(jnp.logical_not(active))
    def _():
        to_sibling.start()

    pl.semaphore_wait(wide_sem, 2)

    @pl.when(active)
    def _():
        pltpu.make_async_copy(pse.at[my], ybuf.at[slot], y_recv.at[slot]).start()
        for s in range(NC * NY):
            pltpu.make_async_copy(pse.at[0], ybuf.at[s], y_recv.at[s]).wait()
        summed = ybuf[0]
        for s in range(1, NC * NY):
            summed = summed + ybuf[s]
        chunk[...] = summed.astype(BF16)
        for k, d in enumerate(z_offsets):
            remote(chunk, zbuf.at[mh, li], z_send.at[k], z_recv.at[mh, li], device(z=at_z(d))).start()
        pltpu.make_async_copy(chunk, zbuf.at[mh, li], z_recv.at[mh, li]).start()

    for copy in x_copies + l_copies + y_copies:
        copy.wait_send()

    @pl.when(jnp.logical_not(active))
    def _():
        to_sibling.wait_send()

    @pl.when(active)
    def _():
        for d in range(1, NL):
            remote(vel.at[1], mombuf.at[li], m_send.at[d], m_recv.at[li], sibling).wait_send()

    for i in range(LPC):
        pltpu.make_async_copy(vel.at[1], mombuf.at[i], m_recv.at[i]).wait()
    for h in range(NH):
        for i in range(LPC):
            pltpu.make_async_copy(chunk, zbuf.at[h, i], z_recv.at[h, i]).wait()
    summed = zbuf[0].astype(F32)
    for h in range(1, NH):
        summed = summed + zbuf[h].astype(F32)
    averaged = summed / (NH * NY * NC)
    velocity = NESTEROV * mombuf[...] + averaged
    outer_step = (averaged + NESTEROV * velocity).astype(BF16)
    half = pl.ds(mc * LPC, LPC)
    og[half, mx, my] = outer_step
    vel[2:] = velocity

    own = og.at[half, mx, my]
    g_copies, f_copies = [], []
    for k, (dx, dy) in enumerate(xy_offsets):
        g_copies.append(remote(own, own, g_send.at[k], g_recv.at[k], device(x=at_x(dx), y=at_y(dy))))
        g_copies[k].start()
        if k == 0:
            f_copies.append(remote(own, own, f_send.at[k], f_recv.at[k], device(x=at_x(dx), y=at_y(dy), c=1 - mc)))
            f_copies[0].start()
    f_copies.append(remote(own, own, f_send.at[NX * NY - 1], f_recv.at[NX * NY - 1], sibling))
    f_copies[1].start()

    @pl.when(active)
    def _():
        pltpu.make_async_copy(vel.at[2 + li], vout.at[my], v_recv.at[my]).start()
        for d in range(1, NY):
            for c in range(NC):
                remote(vel.at[2 + li], vout.at[my], v_send.at[d, c], v_recv.at[my], device(y=at_y(d), c=c)).start()
        remote(vel.at[2 + li], vout.at[my], v_send.at[0, 0], v_recv.at[my], sibling).start()
        for k in range(NZ - 1):
            remote(chunk, zbuf.at[mh, li], z_send.at[k], z_recv.at[mh, li], sibling).wait_send()

    for k in reversed(range(NX * NY - 1)):
        g_copies[k].wait_recv()
        if k > 0:
            dx, dy = xy_offsets[k]
            src = og.at[half, at_x(NX - dx), at_y(NY - dy)]
            copy = remote(src, src, f_send.at[k], f_recv.at[k], sibling)
            copy.start()
            f_copies.append(copy)
    for copy in g_copies:
        copy.wait_send()
    for y in range(NY):
        pltpu.make_async_copy(vel.at[2], vout.at[y], v_recv.at[y]).wait()

    @pl.when(active)
    def _():
        for d in range(1, NY):
            for c in range(NC):
                remote(vel.at[2], vout.at[my], v_send.at[d, c], v_recv.at[my], sibling).wait_send()
        remote(vel.at[2], vout.at[my], v_send.at[0, 0], v_recv.at[my], sibling).wait_send()

    for copy in f_copies:
        copy.wait_send()
    for copy in f_copies:
        copy.wait_recv()


def update_kernel(proj, step, velocity, update_out, velocity_out, update, sem):
    blocks = proj.shape[0] // UPDATE_ROWS
    stores = [pltpu.make_async_copy(velocity, velocity_out, sem.at[blocks])]
    stores[0].start()
    for i in range(blocks):
        rows = pl.ds(i * UPDATE_ROWS, UPDATE_ROWS)
        update[rows] = (OUTER_RATE * jnp.dot(proj[rows], step[...], preferred_element_type=F32)).astype(BF16)
        copy = pltpu.make_async_copy(update.at[rows], update_out.at[rows], sem.at[i])
        copy.start()
        stores.append(copy)
    for copy in stores:
        copy.wait()


def exchange(grad_slab, projector, first_moment, second_moment, momentum):
    ff = projector.shape[0]
    cols = grad_slab.shape[2]
    rows = first_moment.shape[1]
    group = rows // NY
    vmem_spec = pl.BlockSpec(memory_space=pltpu.VMEM)
    hbm_spec = pl.BlockSpec(memory_space=pltpu.HBM)
    dma = pltpu.SemaphoreType.DMA
    return pl.pallas_call(
        exchange_kernel,
        name="exchange",
        out_shape=(
            pltpu.VMEM(projector.shape, BF16),
            pltpu.VMEM((NL, NX, NY, group, cols), BF16),
            pltpu.VMEM((NY, group, cols), F32),
        ),
        in_specs=[hbm_spec] * 5,
        out_specs=(vmem_spec,) * 3,
        scratch_shapes=[
            pltpu.VMEM((ff, cols), BF16),
            pltpu.VMEM((1, rows, cols), F32),
            pltpu.VMEM((1, rows, cols), F32),
            pltpu.VMEM((NL, NX, rows, cols), BF16),
            pltpu.VMEM((NL, NX - 1, rows, cols), BF16),
            pltpu.VMEM((NL - 1, rows, cols), BF16),
            pltpu.VMEM((NL, rows, cols), BF16),
            pltpu.VMEM((NY, group, cols), F32),
            pltpu.VMEM((NC * NY, group, cols), F32),
            pltpu.VMEM((group, cols), BF16),
            pltpu.VMEM((NH, LPC, group, cols), BF16),
            pltpu.VMEM((LPC, group, cols), F32),
            pltpu.VMEM((2 + LPC, group, cols), F32),
            dma((8,)),
            dma((NL, NX - 1)), dma((NL, NX - 1)),
            dma((NL - 1,)), dma((NL,)),
            dma((NY,)), dma((NC * NY,)),
            dma((NL,)), dma((LPC,)),
            dma((NZ - 1,)), dma((NH, LPC)),
            dma((NY, NC)), dma((NY,)),
            dma((NX * NY - 1,)), dma((NX * NY - 1,)),
            dma((NX * NY,)), dma((NX * NY,)),
            pltpu.SemaphoreType.REGULAR,
            pltpu.SemaphoreType.REGULAR,
        ],
        compiler_params=pltpu.CompilerParams(collective_id=1, has_side_effects=True, vmem_limit_bytes=24 << 20),
    )(*[pltpu.with_memory_space_constraint(a, pltpu.HBM) for a in (grad_slab, projector, first_moment, second_moment, momentum)])


def local(grad_slab, projector, first_moment, second_moment, momentum):
    ff, ranks = projector.shape
    cols = grad_slab.shape[2]
    rows = first_moment.shape[1]
    proj, step, velocity = exchange(grad_slab, projector, first_moment, second_moment, momentum)
    vmem_spec = pl.BlockSpec(memory_space=pltpu.VMEM)
    any_spec = pl.BlockSpec(memory_space=pl.ANY)
    operands = (proj, step.reshape(ranks, cols), velocity.reshape(rows, cols))
    return pl.pallas_call(
        update_kernel,
        name="update",
        out_shape=(jax.ShapeDtypeStruct((ff, cols), BF16), jax.ShapeDtypeStruct((rows, cols), F32)),
        in_specs=[vmem_spec] * 3,
        out_specs=(any_spec, any_spec),
        scratch_shapes=[pltpu.VMEM((ff, cols), BF16), pltpu.SemaphoreType.DMA((ff // UPDATE_ROWS + 1,))],
        compiler_params=pltpu.CompilerParams(vmem_limit_bytes=16 << 20),
    )(*[pltpu.with_memory_space_constraint(a, pltpu.VMEM) for a in operands])


def solution(mesh):
    in_specs = (
        P("island", "tensor", None),
        P("tensor", None),
        P("island", "tensor", None),
        P("island", "tensor", None),
        P("tensor", None),
    )
    out_specs = (P("tensor", None), P("tensor", None))
    return jax.shard_map(local, mesh=mesh, in_specs=in_specs, out_specs=out_specs, check_vma=False)
```

```python
import jax
import jax.numpy as jnp
from jax import lax
from jax.experimental import pallas as pl
from jax.experimental.pallas import tpu as pltpu
from jax.sharding import PartitionSpec as P

BETA_ONE = 0.9
BETA_TWO = 0.95
EPSILON = 1e-08
NESTEROV = 0.9
OUTER_RATE = 0.7
MESH = pl.DeviceIdType.MESH
BF16 = jnp.bfloat16
F32 = jnp.float32

NX, NL, NY, NH, NC = 4, 4, 4, 4, 2
NZ = NH * NL
LPC = NL // NC
REACH = 2
UPDATE_ROWS = 256


def exchange_kernel(
    grad, proj, first_in, second_in, momentum_in, pv, og, vout, acc,
    gv, fm, sm, part, xbuf, lsend, lbuf, pse, ybuf, chunk, zbuf, mombuf, vel,
    load_sem, x_send, x_recv, l_send, l_recv, y_send, y_recv, m_send, m_recv, z_send, z_recv,
    v_send, v_recv, g_send, g_recv, f_send, f_recv, ring_sem, wide_sem,
):
    rows = fm.shape[1]
    group = rows // NY
    width = NX * rows
    tensor = lax.axis_index("tensor")
    island = lax.axis_index("island")
    mx, ml = lax.rem(tensor, NX), lax.div(tensor, NX)
    mc = lax.rem(island, NC)
    my = lax.rem(lax.div(island, NC), NY)
    mh = lax.div(island, NC * NY)
    mz = mh * NL + ml
    sigma = lax.div(ml, LPC)
    active = mc == sigma
    li = lax.rem(ml, LPC)

    def device(x=mx, y=my, z=mz, c=mc):
        return ((lax.div(z, NL) * NY + y) * NC + c, lax.rem(z, NL) * NX + x)

    def at_x(d):
        return lax.rem(mx + d, NX)

    def at_y(d):
        return lax.rem(my + d, NY)

    def at_l(d):
        return lax.rem(ml + d, NL)

    def at_z(d):
        return lax.rem(mz + d, NZ)

    farthest = jnp.where(ml < 2, 3, 0)
    nearer = 1 + lax.rem(ml, 2)
    order = (farthest, 6 - ml - farthest - nearer, nearer, ml)
    sibling = device(c=1 - mc)
    xy_offsets = sorted(
        [(dx, dy) for dx in range(NX) for dy in range(NY) if (dx, dy) != (0, 0)],
        key=lambda d: (d == (2, 2), -(min(d[0], NX - d[0]) + min(d[1], NY - d[1]))))
    z_offsets = (8, 7, 9, 6, 10, 5, 11, 4, 12, 3, 13, 2, 14, 1, 15)

    def remote(src, dst, send, recv, to):
        return pltpu.make_async_remote_copy(
            src_ref=src, dst_ref=dst, send_sem=send, recv_sem=recv, device_id=to, device_id_type=MESH)

    loads = [pltpu.make_async_copy(grad.at[0], gv, load_sem.at[0])]
    ranks = [pl.ds(pl.multiple_of(block * width, width), width) for block in order]
    for j in range(NL):
        loads.append(pltpu.make_async_copy(proj.at[:, ranks[j]], pv.at[:, ranks[j]], load_sem.at[1 + j]))
    loads.append(pltpu.make_async_copy(first_in, fm, load_sem.at[5]))
    loads.append(pltpu.make_async_copy(second_in, sm, load_sem.at[6]))
    own_rows = pl.ds(pl.multiple_of(my * group, group), group)
    loads.append(pltpu.make_async_copy(momentum_in.at[own_rows], vel.at[0], load_sem.at[7]))
    for j in (0, 1, 5, 6, 7):
        loads[j].start()

    barrier = pltpu.get_barrier_semaphore()
    partners = [device(z=at_z(d)) for d in z_offsets if min(d, NZ - d) <= REACH]
    partners += [device(x=at_x(d)) for d in range(1, NX)]
    partners += [device(y=at_y(d)) for d in range(1, NY)]
    partners += [device(y=at_y(d), c=1 - mc) for d in range(NY)]
    for partner in partners:
        pl.semaphore_signal(barrier, inc=1, device_id=partner, device_id_type=MESH)

    x_copies = []
    loads[0].wait()
    loads[1].wait()
    for j in range(1, NL):
        loads[1 + j].start()
    for j in range(NL):
        if j:
            loads[1 + j].wait()
        block = lax.dot_general(pv[:, ranks[j]], gv[...], (((0,), (0,)), ((), ())), preferred_element_type=F32)
        block = block.astype(BF16)
        part[j] = block.reshape(part.shape[1:])
        if j == 0:
            pl.semaphore_wait(barrier, len(partners))
            for d in (REACH, NZ - REACH):
                pl.semaphore_signal(ring_sem, inc=1, device_id=device(z=at_z(d)), device_id_type=MESH)
        for dx in (2, 1, 3):
            copy = remote(part.at[j, at_x(dx)], xbuf.at[j, dx - 1], x_send.at[j, dx - 1], x_recv.at[j, dx - 1], device(x=at_x(dx)))
            copy.start()
            x_copies.append(copy)

    pl.semaphore_wait(ring_sem, 2)
    for d in (2 * REACH, NZ - 2 * REACH):
        pl.semaphore_signal(wide_sem, inc=1, device_id=device(z=at_z(d)), device_id_type=MESH)

    loads[7].wait()
    vel[1] = vel[0]

    @pl.when(active)
    def _():
        pltpu.make_async_copy(vel.at[1], mombuf.at[li], m_recv.at[li]).start()
        for d in range(1, NL):
            remote(vel.at[1], mombuf.at[li], m_send.at[d], m_recv.at[li], device(z=mz - ml + at_l(d))).start()

    def over_x(j):
        for k in range(3):
            x_copies[3 * j + k].wait_recv()
        total = part[j, mx].astype(F32)
        for k in range(3):
            total = total + xbuf[j, k].astype(F32)
        return total

    l_copies = []
    for j in range(NL - 1):
        lsend[j] = over_x(j).astype(BF16)
        copy = remote(lsend.at[j], lbuf.at[ml], l_send.at[j], l_recv.at[ml], device(z=mz - ml + order[j]))
        copy.start()
        l_copies.append(copy)
    total = over_x(NL - 1)
    loads[5].wait()
    loads[6].wait()
    for d in range(1, NL):
        pltpu.make_async_copy(lsend.at[0], lbuf.at[at_l(d)], l_recv.at[at_l(d)]).wait()
        total = total + lbuf[at_l(d)].astype(F32)

    first = BETA_ONE * fm[0] + (1.0 - BETA_ONE) * total
    second = BETA_TWO * sm[0] + (1.0 - BETA_TWO) * total * total
    pseudo = first / (jnp.sqrt(second) + EPSILON)
    pse[...] = pseudo.reshape(pse.shape)

    slot = mc * NY + my
    y_copies = []
    for d in (2, 1, 3):
        copy = remote(pse.at[at_y(d)], ybuf.at[slot], y_send.at[d], y_recv.at[slot], device(y=at_y(d), c=sigma))
        copy.start()
        y_copies.append(copy)
    to_sibling = remote(pse.at[my], ybuf.at[slot], y_send.at[0], y_recv.at[slot], sibling)

    @pl.when(jnp.logical_not(active))
    def _():
        to_sibling.start()

    pl.semaphore_wait(wide_sem, 2)

    @pl.when(active)
    def _():
        pltpu.make_async_copy(pse.at[my], ybuf.at[slot], y_recv.at[slot]).start()
        for s in range(NC * NY):
            pltpu.make_async_copy(pse.at[0], ybuf.at[s], y_recv.at[s]).wait()
        summed = ybuf[0]
        for s in range(1, NC * NY):
            summed = summed + ybuf[s]
        chunk[...] = summed.astype(BF16)
        for k, d in enumerate(z_offsets):
            remote(chunk, zbuf.at[mh, li], z_send.at[k], z_recv.at[mh, li], device(z=at_z(d))).start()
        pltpu.make_async_copy(chunk, zbuf.at[mh, li], z_recv.at[mh, li]).start()

    for copy in x_copies + l_copies + y_copies:
        copy.wait_send()

    @pl.when(jnp.logical_not(active))
    def _():
        to_sibling.wait_send()

    @pl.when(active)
    def _():
        for d in range(1, NL):
            remote(vel.at[1], mombuf.at[li], m_send.at[d], m_recv.at[li], sibling).wait_send()

    for i in range(LPC):
        pltpu.make_async_copy(vel.at[1], mombuf.at[i], m_recv.at[i]).wait()
    for h in range(NH):
        for i in range(LPC):
            pltpu.make_async_copy(chunk, zbuf.at[h, i], z_recv.at[h, i]).wait()
    summed = zbuf[0].astype(F32)
    for h in range(1, NH):
        summed = summed + zbuf[h].astype(F32)
    averaged = summed / (NH * NY * NC)
    velocity = NESTEROV * mombuf[...] + averaged
    outer_step = (averaged + NESTEROV * velocity).astype(BF16)
    half = pl.ds(mc * LPC, LPC)
    og[half, mx, my] = outer_step
    vel[2:] = velocity

    own = og.at[half, mx, my]
    g_copies, f_copies = [], []
    for k, (dx, dy) in enumerate(xy_offsets):
        g_copies.append(remote(own, own, g_send.at[k], g_recv.at[k], device(x=at_x(dx), y=at_y(dy))))
        g_copies[k].start()
        if k == NX * NY - 2:
            f_copies.append(remote(own, own, f_send.at[k], f_recv.at[k], device(x=at_x(dx), y=at_y(dy), c=1 - mc)))
            f_copies[0].start()
    f_copies.append(remote(own, own, f_send.at[NX * NY - 1], f_recv.at[NX * NY - 1], sibling))
    f_copies[1].start()

    @pl.when(active)
    def _():
        pltpu.make_async_copy(vel.at[2 + li], vout.at[my], v_recv.at[my]).start()
        for d in range(1, NY):
            for c in range(NC):
                remote(vel.at[2 + li], vout.at[my], v_send.at[d, c], v_recv.at[my], device(y=at_y(d), c=c)).start()
        remote(vel.at[2 + li], vout.at[my], v_send.at[0, 0], v_recv.at[my], sibling).start()
        for k in range(NZ - 1):
            remote(chunk, zbuf.at[mh, li], z_send.at[k], z_recv.at[mh, li], sibling).wait_send()

    for k in [*reversed(range(NX * NY - 2)), NX * NY - 2]:
        g_copies[k].wait_recv()
        if k < NX * NY - 2:
            dx, dy = xy_offsets[k]
            src = og.at[half, at_x(NX - dx), at_y(NY - dy)]
            copy = remote(src, src, f_send.at[k], f_recv.at[k], sibling)
            copy.start()
            f_copies.append(copy)
    near = og[half].reshape(LPC * width, og.shape[-1])
    for i in range(acc.shape[0] // UPDATE_ROWS):
        block = pl.ds(i * UPDATE_ROWS, UPDATE_ROWS)
        acc[block] = jnp.dot(pv[block, pl.ds(pl.multiple_of(mc * LPC * width, LPC * width), LPC * width)], near, preferred_element_type=F32)
    for copy in g_copies:
        copy.wait_send()
    for y in range(NY):
        pltpu.make_async_copy(vel.at[2], vout.at[y], v_recv.at[y]).wait()

    @pl.when(active)
    def _():
        for d in range(1, NY):
            for c in range(NC):
                remote(vel.at[2], vout.at[my], v_send.at[d, c], v_recv.at[my], sibling).wait_send()
        remote(vel.at[2], vout.at[my], v_send.at[0, 0], v_recv.at[my], sibling).wait_send()

    for copy in f_copies:
        copy.wait_send()
    for copy in f_copies:
        copy.wait_recv()


def update_kernel(proj, step, velocity, acc, update_out, velocity_out, update, sem):
    ranks = step.shape[0] // NC
    far = pl.ds(pl.multiple_of((1 - lax.rem(lax.axis_index("island"), NC)) * ranks, ranks), ranks)
    rest = step[far]
    blocks = proj.shape[0] // UPDATE_ROWS
    stores = [pltpu.make_async_copy(velocity, velocity_out, sem.at[blocks])]
    stores[0].start()
    for i in range(blocks):
        rows = pl.ds(i * UPDATE_ROWS, UPDATE_ROWS)
        update[rows] = (OUTER_RATE * (acc[rows] + jnp.dot(proj[rows, far], rest, preferred_element_type=F32))).astype(BF16)
        copy = pltpu.make_async_copy(update.at[rows], update_out.at[rows], sem.at[i])
        copy.start()
        stores.append(copy)
    for copy in stores:
        copy.wait()


def exchange(grad_slab, projector, first_moment, second_moment, momentum):
    ff = projector.shape[0]
    cols = grad_slab.shape[2]
    rows = first_moment.shape[1]
    group = rows // NY
    vmem_spec = pl.BlockSpec(memory_space=pltpu.VMEM)
    hbm_spec = pl.BlockSpec(memory_space=pltpu.HBM)
    dma = pltpu.SemaphoreType.DMA
    return pl.pallas_call(
        exchange_kernel,
        name="exchange",
        out_shape=(
            pltpu.VMEM(projector.shape, BF16),
            pltpu.VMEM((NL, NX, NY, group, cols), BF16),
            pltpu.VMEM((NY, group, cols), F32),
            pltpu.VMEM((ff, cols), F32),
        ),
        in_specs=[hbm_spec] * 5,
        out_specs=(vmem_spec,) * 4,
        scratch_shapes=[
            pltpu.VMEM((ff, cols), BF16),
            pltpu.VMEM((1, rows, cols), F32),
            pltpu.VMEM((1, rows, cols), F32),
            pltpu.VMEM((NL, NX, rows, cols), BF16),
            pltpu.VMEM((NL, NX - 1, rows, cols), BF16),
            pltpu.VMEM((NL - 1, rows, cols), BF16),
            pltpu.VMEM((NL, rows, cols), BF16),
            pltpu.VMEM((NY, group, cols), F32),
            pltpu.VMEM((NC * NY, group, cols), F32),
            pltpu.VMEM((group, cols), BF16),
            pltpu.VMEM((NH, LPC, group, cols), BF16),
            pltpu.VMEM((LPC, group, cols), F32),
            pltpu.VMEM((2 + LPC, group, cols), F32),
            dma((8,)),
            dma((NL, NX - 1)), dma((NL, NX - 1)),
            dma((NL - 1,)), dma((NL,)),
            dma((NY,)), dma((NC * NY,)),
            dma((NL,)), dma((LPC,)),
            dma((NZ - 1,)), dma((NH, LPC)),
            dma((NY, NC)), dma((NY,)),
            dma((NX * NY - 1,)), dma((NX * NY - 1,)),
            dma((NX * NY,)), dma((NX * NY,)),
            pltpu.SemaphoreType.REGULAR,
            pltpu.SemaphoreType.REGULAR,
        ],
        compiler_params=pltpu.CompilerParams(collective_id=1, has_side_effects=True, vmem_limit_bytes=24 << 20),
    )(*[pltpu.with_memory_space_constraint(a, pltpu.HBM) for a in (grad_slab, projector, first_moment, second_moment, momentum)])


def local(grad_slab, projector, first_moment, second_moment, momentum):
    ff, ranks = projector.shape
    cols = grad_slab.shape[2]
    rows = first_moment.shape[1]
    proj, step, velocity, acc = exchange(grad_slab, projector, first_moment, second_moment, momentum)
    vmem_spec = pl.BlockSpec(memory_space=pltpu.VMEM)
    any_spec = pl.BlockSpec(memory_space=pl.ANY)
    operands = (proj, step.reshape(ranks, cols), velocity.reshape(rows, cols), acc)
    return pl.pallas_call(
        update_kernel,
        name="update",
        out_shape=(jax.ShapeDtypeStruct((ff, cols), BF16), jax.ShapeDtypeStruct((rows, cols), F32)),
        in_specs=[vmem_spec] * 4,
        out_specs=(any_spec, any_spec),
        scratch_shapes=[pltpu.VMEM((ff, cols), BF16), pltpu.SemaphoreType.DMA((ff // UPDATE_ROWS + 1,))],
        compiler_params=pltpu.CompilerParams(vmem_limit_bytes=16 << 20),
    )(*[pltpu.with_memory_space_constraint(a, pltpu.VMEM) for a in operands])


def solution(mesh):
    in_specs = (
        P("island", "tensor", None),
        P("tensor", None),
        P("island", "tensor", None),
        P("island", "tensor", None),
        P("tensor", None),
    )
    out_specs = (P("tensor", None), P("tensor", None))
    return jax.shard_map(local, mesh=mesh, in_specs=in_specs, out_specs=out_specs, check_vma=False)
```
